512 devices in a mesh: dp: 32 (over z, x_hi), point: 16 (over y, x_lo, core).
Axes of the slice: x: 4 (x_hi: 2, x_lo: 2; x = x_hi * 2 + x_lo), y: 4, z: 16, core: 2. Of those that a mesh axis runs over, the one named last changes fastest.
Arguments:
- points: bfloat16 [32, 2, 4096, 512], P('dp', None, 'point'), may hold values from -6 to 6
- hilbert_rank: int32 [32, 2, 4096], P('dp', None, 'point'), may hold values from 0 to 4095, as said below
- patch_id: int32 [32, 2, 4096], P('dp', None, 'point'), may hold values from 0 to 31, never falling along the last dimension, each value on 1 to 256 neighbouring positions
- w_qkv: bfloat16 [512, 1536], replicated, may hold values from -8 to 8
- w_out: bfloat16 [512, 512], replicated, may hold values from -0.25 to 0.25
- w_up: bfloat16 [2048, 512], P('point'), may hold values from -0.25 to 0.25
- w_down: bfloat16 [2048, 512], P('point'), may hold values from -0.125 to 0.125
- cotangent: bfloat16 [32, 2, 4096, 512], P('dp', None, 'point'), may hold values from -0.0234375 to 0.0234375
Outputs:
- layer_out: bfloat16 [32, 2, 4096, 512], P('dp', None, 'point')
- grad_down: float32 [2048, 512], P('point')
The draws below stay inside these ranges and needn't reach their ends.
Inputs may be any that keep to these rules, and one draw needn't show every extreme that they name: `hilbert_rank`: within each cloud the values are a permutation of 0 to 4095. At most 32 points of one device's block of 256 points in Z order have their Hilbert position in one device's block; every Z block sends exactly 32 points to one Hilbert block. `patch_id`: patches are runs of 1 to 256 positions.
All inputs are finite; a program needn't handle non-finite values.
Results may differ from the reference program's by a relative error of at most 0.024.
Values may be sent and summed in bfloat16 or wider, within the bound.
No kernel may reach another device: no remote copies, remote signals or barrier semaphores. Data moves between devices by JAX's collectives and lax.ppermute only.
A program may use at most 64 MiB of HBM per device.

```python
import math
from functools import partial
import jax
import jax.numpy as jnp
import numpy as np
from jax import lax

D = 512
HEADS = 8
FF = 2048
PATCH = 256
MB = 2
PTS_DEV = 256
POINTS = 4096
GROUPS = 32
OVERLAY_LIMIT = 32
N_DP = 32
N_POINT = 16


def one_cloud(key):
    heavy_key, weight_key, row_key, col_key, shuffle_key, order_key = jax.random.split(key, 6)
    indices = jnp.arange(N_POINT, dtype=jnp.int32)
    heavy = jax.random.randint(heavy_key, (), 0, N_POINT, dtype=jnp.int32)
    raw = jax.random.randint(weight_key, (N_POINT,), 900, 1001, dtype=jnp.int32)
    lighter_device = indices != heavy
    others = jnp.where(lighter_device, raw, 0)
    remain = PTS_DEV - OVERLAY_LIMIT
    device_portion = others * remain // jnp.sum(others)
    remaining_points = remain - jnp.sum(device_portion)
    point_position = jnp.cumsum(lighter_device.astype(jnp.int32)) - 1
    extra_points = (lighter_device & (point_position < remaining_points)).astype(jnp.int32)
    point_allotment = device_portion + extra_points + jnp.where(lighter_device, 0, OVERLAY_LIMIT)
    bounds = jnp.cumsum(point_allotment)
    slots = jnp.arange(PTS_DEV, dtype=jnp.int32)
    shift = jnp.sum((slots[:, None] >= bounds[None, :]).astype(jnp.int32), axis=1)
    row_perm = jax.random.permutation(row_key, N_POINT).astype(jnp.int32)
    col_perm = jax.random.permutation(col_key, N_POINT).astype(jnp.int32)
    col_inverse = jnp.argsort(col_perm).astype(jnp.int32)
    target = col_inverse[(shift[None, :] - row_perm[:, None]) % N_POINT]
    sub_keys = jax.random.split(shuffle_key, N_POINT)
    shuffle = jax.vmap(local_order)(sub_keys)
    z_index = indices[:, None] * PTS_DEV + shuffle
    target_of_z = jnp.zeros((POINTS,), jnp.int32).at[z_index.reshape(-1)].set(target.reshape(-1))
    tiebreak = jax.random.permutation(order_key, POINTS).astype(jnp.int32)
    score = target_of_z * POINTS + tiebreak
    order = jnp.argsort(score).astype(jnp.int32)
    return jnp.argsort(order).astype(jnp.int32)


def local_order(subkey):
    return jax.random.permutation(subkey, PTS_DEV).astype(jnp.int32)


def draw_hilbert_rank(key, part):
    key = jax.random.fold_in(key, 7)
    cloud_keys = jax.random.split(key, N_DP * MB)
    ranks = jax.vmap(one_cloud)(cloud_keys)
    return ranks.reshape(N_DP, MB, POINTS)


def draw_w_qkv(key, part):
    key = jax.random.fold_in(key, 11)
    base_key = jax.random.fold_in(key, 0)
    limit = 5.0 * D ** (-0.5)
    base = jnp.clip(jax.random.normal(base_key, (D, 3 * D), jnp.float32) * D ** (-0.5), -limit, limit)
    return base.astype(jnp.bfloat16)


def level_of(stream_key, extent, cuts, low, top_value):
    gain = 1.0
    for position, parts in cuts:
        steps = jax.random.uniform(jax.random.fold_in(jax.random.fold_in(stream_key, 6), position), (parts,), jnp.float32, low / len(cuts), top_value / len(cuts))
        gain = gain * jnp.repeat(jnp.exp(steps), extent[position] // parts).reshape((-1,) + (1,) * (len(extent) - 1 - position))
    return gain


def profile(number_of, total, most, skew):
    portions = [(1 << 20) // math.isqrt(grade ** skew) + 1 for grade in range(2, number_of + 1)]
    spare, given = total - most - (number_of - 1), [1] * (number_of - 1)
    while spare > 0:
        candidates = [i for i in range(number_of - 1) if given[i] < most]
        pool, left = sum([portions[i] for i in candidates]), spare
        for i in candidates:
            more = min(most - given[i], max(1, left * portions[i] // pool), spare)
            given[i] = given[i] + more
            spare = spare - more
    return np.array([most] + given)


def ragged_sizes(stream_key, number_of, total, bound, lean):
    if number_of == 2:
        one = jax.random.randint(stream_key, (), max(1, total - bound), min(bound, total - 1) + 1)
        return jnp.stack([one, total - one])
    lengths = jnp.asarray(profile(number_of, total, bound, lean), jnp.int32)
    pairs = (number_of - 1) // 2
    donor, receiver = lengths[1:1 + 2 * pairs:2], lengths[2:2 + 2 * pairs:2]
    slack = jnp.minimum(donor - 1, bound - receiver)
    shifted = jax.random.randint(jax.random.fold_in(stream_key, 1), (pairs,), 0, 1 << 20) % (slack + 1)
    lengths = lengths.at[1:1 + 2 * pairs:2].set(donor - shifted).at[2:2 + 2 * pairs:2].set(receiver + shifted)
    return lengths[jax.random.permutation(jax.random.fold_in(stream_key, 2), number_of)]


def gaussian(rng, shape, deviation, most, cuts=(), kind=jnp.bfloat16):
    drawn = deviation * jax.random.normal(rng, shape, jnp.float32)
    if cuts:
        drawn = drawn * level_of(rng, shape, cuts, -0.22, 0.18)
    return jnp.clip(drawn, -most, most).astype(kind)


def setup_inputs(seed: int = 0) -> dict:
    streams_of = jax.random.split(jax.random.key(seed), 9)
    points = gaussian(streams_of[0], (GROUPS, MB, POINTS, D), 1.0, 6.0, ((0, 32), (2, 16)))
    hilbert_rank = draw_hilbert_rank(jax.random.fold_in(streams_of[8], 71), 0)
    patch_id = jax.vmap(lambda own: jnp.searchsorted(jnp.cumsum(ragged_sizes(own, 2 * POINTS // PATCH, POINTS, PATCH, 0)), jnp.arange(POINTS), side="right"))(jax.random.split(streams_of[2], GROUPS * MB)).reshape((GROUPS, MB, POINTS)).astype(jnp.int32)
    w_qkv = draw_w_qkv(jax.random.fold_in(streams_of[8], 71), 0)
    w_out = gaussian(streams_of[4], (D, D), D ** -0.5, 0.25)
    w_up = gaussian(streams_of[5], (FF, D), D ** -0.5, 0.25, ((0, 16),))
    w_down = gaussian(streams_of[6], (FF, D), FF ** -0.5, 0.125, ((0, 16),))
    cotangent = gaussian(streams_of[7], (GROUPS, MB, POINTS, D), (2.0 * (GROUPS * MB * POINTS) ** -0.5), 0.0234375, ((0, 32), (2, 16)))
    return {"points": points, "hilbert_rank": hilbert_rank, "patch_id": patch_id, "w_qkv": w_qkv, "w_out": w_out, "w_up": w_up, "w_down": w_down, "cotangent": cotangent}


def normalize(values):
    wide = values.astype(jnp.float32)
    centre = lax.optimization_barrier(jnp.mean(wide, axis=-1, keepdims=True))
    spread = lax.optimization_barrier(jnp.mean(jnp.square(wide - centre), axis=-1, keepdims=True))
    return ((wide - centre) * lax.rsqrt(spread + 1e-05)).astype(jnp.bfloat16)

def attend(queries, query_tags, keyvals, key_tags):
    batch, length, width = queries.shape
    head_size = width // HEADS
    query_heads = queries.reshape(batch, length, HEADS, head_size).astype(jnp.float32)
    key_heads = keyvals[..., :width].reshape(batch, -1, HEADS, head_size).astype(jnp.float32)
    value_heads = keyvals[..., width:].reshape(batch, -1, HEADS, head_size).astype(jnp.float32)
    scores = jnp.einsum('bqhd,bkhd->bhqk', query_heads, key_heads) * head_size ** (-0.5)
    allowed = query_tags[:, None, :, None] == key_tags[:, None, None, :]
    scores = jnp.where(allowed, scores, -1e+30)
    peak = lax.optimization_barrier(jnp.max(scores, axis=-1, keepdims=True))
    weights = jnp.where(allowed, jnp.exp(scores - peak), 0.0)
    total = lax.optimization_barrier(jnp.sum(weights, axis=-1, keepdims=True))
    probs = (weights / total).astype(jnp.bfloat16)
    mixed = jnp.einsum('bhqk,bkhd->bqhd', probs.astype(jnp.float32), value_heads)
    return mixed.reshape(batch, length, width).astype(jnp.bfloat16)

def place_rows(features, ranks):
    return jnp.zeros_like(features).at[ranks].set(features)

def one_group(weights, grad_total, inputs):
    w_qkv, w_out, w_up, w_down = weights
    features, ranks, patches, upstream = inputs
    ordered = jax.vmap(place_rows)(features, ranks)
    normed = normalize(ordered)
    projected = jnp.dot(normed.reshape(-1, D), w_qkv, preferred_element_type=jnp.float32)
    projected = projected.astype(jnp.bfloat16).reshape(MB, POINTS, 3 * D)
    queries = projected[..., :D]
    keyvals = projected[..., D:]
    tags = patches + 1
    padded_kv = jnp.pad(keyvals, ((0, 0), (PATCH, PATCH), (0, 0)))
    padded_tags = jnp.pad(tags, ((0, 0), (PATCH, PATCH)))

    def block(index):
        start = (index * PTS_DEV).astype(jnp.int32)
        block_q = lax.dynamic_slice_in_dim(queries, start, PTS_DEV, 1)
        block_t = lax.dynamic_slice_in_dim(tags, start, PTS_DEV, 1)
        block_kv = lax.dynamic_slice_in_dim(padded_kv, start, PTS_DEV + 2 * PATCH, 1)
        block_kt = lax.dynamic_slice_in_dim(padded_tags, start, PTS_DEV + 2 * PATCH, 1)
        return attend(block_q, block_t, block_kv, block_kt)
    blocks = lax.map(block, jnp.arange(N_POINT, dtype=jnp.int32))
    attended = jnp.transpose(blocks, (1, 0, 2, 3)).reshape(MB * POINTS, D)
    flat_in = ordered.reshape(MB * POINTS, D)
    residual = (flat_in.astype(jnp.float32) + jnp.dot(attended, w_out, preferred_element_type=jnp.float32)).astype(jnp.bfloat16)
    normed_two = normalize(residual)
    hidden = jax.nn.gelu(lax.dot_general(normed_two, w_up, (((1,), (1,)), ((), ())), preferred_element_type=jnp.float32)).astype(jnp.bfloat16)
    mixed = jnp.dot(hidden, w_down, preferred_element_type=jnp.float32)
    layer_out = (residual.astype(jnp.float32) + mixed).astype(jnp.bfloat16).reshape(MB, POINTS, D)
    hidden_blocks = hidden.reshape(MB, POINTS, FF)

    def add_block(total, index):
        start = (index * PTS_DEV).astype(jnp.int32)
        picked = lax.dynamic_slice_in_dim(hidden_blocks, start, PTS_DEV, 1).reshape(MB * PTS_DEV, FF)
        cot_rows = lax.dynamic_slice_in_dim(upstream, start, PTS_DEV, 1).reshape(MB * PTS_DEV, D)
        term = lax.dot_general(picked, cot_rows, (((0,), (0,)), ((), ())), preferred_element_type=jnp.float32)
        return (total + term.astype(jnp.bfloat16).astype(jnp.float32), None)
    grad_total, _ = lax.scan(add_block, grad_total, jnp.arange(N_POINT, dtype=jnp.int32))
    return (grad_total, layer_out)

def reference(points, hilbert_rank, patch_id, w_qkv, w_out, w_up, w_down, cotangent):
    start_grad = jnp.zeros((FF, D), jnp.float32)
    step_fn = partial(one_group, (w_qkv, w_out, w_up, w_down))
    grad_down, layer_out = lax.scan(step_fn, start_grad, (points, hilbert_rank, patch_id, cotangent))
    return (layer_out, grad_down)
```

```python
import math

import jax
import jax.numpy as jnp
from jax import lax
from jax.experimental import pallas as pl
from jax.experimental.pallas import tpu as pltpu
from jax.sharding import PartitionSpec as P

HEADS = 8
LANES = 128
TAG_ROWS = 16
LOG2E = math.log2(math.e)
PARAMS = pltpu.CompilerParams(vmem_limit_bytes=48 * 1024 * 1024)
F32 = jnp.float32
BF16 = jnp.bfloat16


def dot(a, b, dims=((1,), (0,))):
    return lax.dot_general(a, b, (dims, ((), ())), preferred_element_type=F32)


def normalize(wide):
    centre = jnp.mean(wide, axis=-1, keepdims=True)
    spread = jnp.mean(jnp.square(wide - centre), axis=-1, keepdims=True)
    return ((wide - centre) * lax.rsqrt(spread + 1e-05)).astype(BF16)


def column(row):
    return jnp.transpose(jnp.broadcast_to(row, (LANES, row.shape[1])))


def dispatch_kernel(ranks_ref, points_ref, out_ref):
    clouds, length, width = points_ref.shape
    devices, _, capacity, _ = out_ref.shape
    ranks = ranks_ref[...]
    target = ranks // length
    local = ranks - target * length
    before = (
        lax.broadcasted_iota(jnp.int32, (length, length), 0)
        < lax.broadcasted_iota(jnp.int32, (length, length), 1)
    ).astype(F32).astype(BF16)
    for c in range(clouds):
        goes = lax.broadcasted_iota(jnp.int32, (devices, length), 0) == target[c : c + 1]
        ones = goes.astype(F32)
        earlier = dot(ones.astype(BF16), before)
        slot = jnp.sum(earlier * ones, axis=0, keepdims=True).astype(jnp.int32)
        where_to = target[c : c + 1] * capacity + slot
        pick = (
            lax.broadcasted_iota(jnp.int32, (devices * capacity, length), 0) == where_to
        ).astype(F32).astype(BF16)
        places = column((local[c : c + 1] + 1).astype(F32)).astype(BF16)
        rows = dot(pick, points_ref[c]).astype(BF16)
        marks = dot(pick, places).astype(BF16)
        out_ref[:, c, :, :width] = rows.reshape(devices, capacity, width)
        out_ref[:, c, :, width:] = marks.reshape(devices, capacity, LANES)


def project_kernel(arrived_ref, tags_ref, w_ref, ordered_ref, halo_ref, qkv_ref):
    devices, clouds, capacity, _ = arrived_ref.shape
    _, length, width = ordered_ref.shape
    slots = devices * capacity
    for c in range(clouds):
        rows = arrived_ref[:, c, :, :width].reshape(slots, width)
        marks = arrived_ref[:, c, :, width:].reshape(slots, LANES).astype(F32)
        wide_marks = jnp.concatenate([marks] * (length // LANES), axis=1)
        here = lax.broadcasted_iota(jnp.int32, (slots, length), 1).astype(F32) + 1.0
        put = (wide_marks == here).astype(F32).astype(BF16)
        ordered = dot(put, rows, ((0,), (0,)))
        ordered_ref[c] = ordered.astype(BF16)
        normed = normalize(ordered)
        halo_ref[c, :length] = normed
        tag_row = jnp.concatenate(
            [tags_ref[c : c + 1].astype(F32) + 1.0, jnp.zeros((1, width - length), F32)], axis=1
        )
        halo_ref[c, length:] = jnp.broadcast_to(tag_row, (TAG_ROWS, width)).astype(BF16)
        qkv_ref[c] = dot(normed, w_ref[...]).astype(BF16)


def attend_kernel(qkv_ref, low_ref, high_ref, halo_ref, ordered_ref, w_ref, w_out_ref, res_ref, normed_ref):
    clouds, length, width = ordered_ref.shape
    head = width // HEADS
    pair = LANES // head
    first = lax.broadcasted_iota(jnp.int32, (length, LANES), 1) < head
    ones = jnp.ones((length, LANES), BF16)
    scale = head ** (-0.5) * LOG2E
    for c in range(clouds):
        own_tags = halo_ref[c, length : length + TAG_ROWS, :length].astype(F32)[:1]
        asks = column(own_tags)
        asks = jnp.concatenate([asks] * (length // LANES), axis=1)
        sides = []
        for ref in (low_ref, high_ref):
            kv = dot(ref[c, :length], w_ref[:, width:]).astype(BF16)
            sides.append((kv, ref[c, length : length + TAG_ROWS, :length].astype(F32)[:1]))
        sides.append((qkv_ref[c, :, width:], own_tags))
        allowed = [asks == tags for _, tags in sides]
        for h in range(HEADS // pair):
            lanes = slice(h * LANES, (h + 1) * LANES)
            values = slice(width + h * LANES, width + (h + 1) * LANES)
            queries = qkv_ref[c, :, lanes]
            mixed = []
            for inside in (first, ~first):
                asked = jnp.where(inside, queries, jnp.zeros_like(queries))
                scores = [
                    jnp.where(ok, dot(asked, kv[:, lanes], ((1,), (1,))), -1e30)
                    for (kv, _), ok in zip(sides, allowed)
                ]
                peak = jnp.max(
                    jnp.maximum(jnp.maximum(scores[0], scores[1]), scores[2]), axis=1, keepdims=True
                )
                total = None
                for (kv, _), s in zip(sides, scores):
                    weights = jnp.exp2((s - peak) * scale).astype(BF16)
                    part = dot(weights, jnp.concatenate([kv[:, values], ones], axis=1))
                    total = part if total is None else total + part
                mixed.append(total[:, :LANES] / total[:, LANES:])
            attended = jnp.where(first, mixed[0], mixed[1]).astype(BF16)
            part = dot(attended, w_out_ref[lanes, :])
            out = part if h == 0 else out + part
        residual = (ordered_ref[c].astype(F32) + out).astype(BF16)
        rows = slice(c * length, (c + 1) * length)
        res_ref[rows] = residual
        normed_ref[rows] = normalize(residual.astype(F32))


def up_kernel(parity_ref, normed_ref, w_up_ref, cot_ref, hidden_ref, grad_ref):
    blocks, _, units, _ = w_up_ref.shape
    parity = parity_ref[0]
    half = units // 2
    for j in range(0, blocks, 2):
        weights = w_up_ref[j : j + 2, parity].reshape(2 * units, -1)
        product = dot(weights, normed_ref[...], ((1,), (1,)))
        hidden = jax.nn.gelu(product).astype(BF16)
        hidden_ref[j * units : (j + 2) * units] = hidden
        grad = dot(hidden, cot_ref[...]).astype(BF16)
        for k in range(2):
            grad_ref[0, j + k] = grad[k * units : k * units + half]
            grad_ref[1, j + k] = grad[k * units + half : (k + 1) * units]


def down_kernel(parity_ref, res_ref, one_ref, two_ref, w_down_ref, out_ref):
    blocks, _, units, width = w_down_ref.shape
    parity = parity_ref[0]
    total = dot(one_ref[...], w_down_ref[:, parity].reshape(blocks * units, width), ((0,), (0,)))
    total += dot(two_ref[...], w_down_ref[:, 1 - parity].reshape(blocks * units, width), ((0,), (0,)))
    out_ref[...] = (res_ref[...].astype(F32) + total).astype(BF16)


VMEM = pl.BlockSpec(memory_space=pltpu.VMEM)
SMEM = pl.BlockSpec(memory_space=pltpu.SMEM)


def call(kernel, outs, args, scalars=0, flops=0):
    return pl.pallas_call(
        kernel,
        out_shape=[jax.ShapeDtypeStruct(shape, BF16) for shape in outs],
        in_specs=[SMEM] * scalars + [VMEM] * (len(args) - scalars),
        out_specs=[VMEM] * len(outs),
        compiler_params=PARAMS,
        cost_estimate=pl.CostEstimate(
            flops=flops, bytes_accessed=sum(2 * math.prod(s) for s in outs) * 2, transcendentals=0
        ),
    )(*args)


def on_device(points, hilbert_rank, patch_id, w_qkv, w_out, w_up, w_down, cotangent):
    clouds, length, width = points.shape[1:]
    rows_all = clouds * length
    devices = lax.axis_size("point")
    groups = lax.axis_size("dp")
    units = w_up.shape[0]
    capacity = 2 * length // devices
    me = lax.axis_index("point")
    parity = (me & 1).reshape(1).astype(jnp.int32)
    up_all = lax.all_gather(w_up, "point", axis=0, tiled=True)
    down_all = lax.all_gather(w_down, "point", axis=0, tiled=True)

    (outgoing,) = call(
        dispatch_kernel,
        [(devices, clouds, capacity, width + LANES)],
        (hilbert_rank[0], points[0]),
        flops=4 * rows_all * devices * capacity * width // clouds,
    )
    arrived = lax.all_to_all(outgoing, "point", 0, 0, tiled=True)
    ordered, halo, qkv = call(
        project_kernel,
        [(clouds, length, width), (clouds, length + TAG_ROWS, width), (clouds, length, 3 * width)],
        (arrived, patch_id[0], w_qkv),
        flops=2 * rows_all * width * 4 * width,
    )
    forward = [(i, i + 1) for i in range(devices - 1)]
    backward = [(i + 1, i) for i in range(devices - 1)]
    low = lax.ppermute(halo, "point", forward)
    high = lax.ppermute(halo, "point", backward)
    residual, normed_two = call(
        attend_kernel,
        [(rows_all, width), (rows_all, width)],
        (qkv, low, high, halo, ordered, w_qkv, w_out),
        flops=2 * rows_all * width * (4 * width + 12 * length),
    )

    blocks = devices // 2
    halves = [(blocks * units, rows_all), (2, blocks, units // 2, width)]
    up_blocks = up_all.reshape(blocks, 2, units, width)
    cot_rows = cotangent[0].reshape(rows_all, width)
    up_flops = 4 * rows_all * width * units * blocks
    hidden_two, grad_two = call(
        up_kernel, halves, (1 - parity, normed_two, up_blocks, cot_rows), 1, up_flops
    )
    grad_got = lax.ppermute(grad_two, "point", [(i, i ^ 1) for i in range(devices)])
    hidden_one, grad_one = call(
        up_kernel, halves, (parity, normed_two, up_blocks, cot_rows), 1, up_flops
    )
    grad = (grad_one.astype(F32) + grad_got.astype(F32)).astype(BF16)
    grad = grad.reshape(2 * blocks, units // 2, width)

    stages = groups // 2
    planes = [
        [(z * 2 + h) * devices + j * 2 + core for h in range(2) for j in range(blocks)]
        for z in range(stages)
        for core in range(2)
    ]
    grad = lax.all_to_all(
        grad, ("dp", "point"), 0, 0, axis_index_groups=planes, tiled=True
    )
    grad = jnp.sum(grad.astype(F32), axis=0).astype(BF16)
    piece = units // groups
    grad = lax.all_to_all(
        grad.reshape(stages, piece, width),
        "dp",
        0,
        0,
        axis_index_groups=[[z * 2 + h for z in range(stages)] for h in range(2)],
        tiled=True,
    )
    grad = jnp.sum(grad.astype(F32), axis=0).astype(BF16)
    grad = lax.all_to_all(
        jnp.broadcast_to(grad[None], (groups, piece, width)), "dp", 0, 0, tiled=True
    )
    grad = grad.reshape(stages, 2, piece, width).transpose(1, 0, 2, 3).reshape(units, width)
    grad_down = grad.astype(F32)

    (layer_out,) = call(
        down_kernel,
        [(rows_all, width)],
        (parity, residual, hidden_one, hidden_two, down_all.reshape(blocks, 2, units, width)),
        1,
        2 * rows_all * width * devices * units,
    )
    return layer_out.reshape(1, clouds, length, width), grad_down


def solution(mesh):
    placed = (
        P("dp", None, "point", None),
        P("dp", None, "point"),
        P("dp", None, "point"),
        P(),
        P(),
        P("point", None),
        P("point", None),
        P("dp", None, "point", None),
    )
    return jax.shard_map(
        on_device,
        mesh=mesh,
        in_specs=placed,
        out_specs=(P("dp", None, "point", None), P("point", None)),
        check_vma=False,
    )
```

```python
import math
from functools import partial

import jax
import jax.numpy as jnp
from jax import lax
from jax.experimental import pallas as pl
from jax.experimental.pallas import tpu as pltpu
from jax.sharding import PartitionSpec as P

HEADS = 8
LANES = 128
TAG_ROWS = 16
LOG2E = math.log2(math.e)
SMALL = 16 * 1024 * 1024
LARGE = 60 * 1024 * 1024
F32 = jnp.float32
BF16 = jnp.bfloat16


def dot(a, b, dims=((1,), (0,))):
    return lax.dot_general(a, b, (dims, ((), ())), preferred_element_type=F32)


def normalize(wide):
    centre = jnp.mean(wide, axis=-1, keepdims=True)
    spread = jnp.mean(jnp.square(wide - centre), axis=-1, keepdims=True)
    return ((wide - centre) * lax.rsqrt(spread + 1e-05)).astype(BF16)


def column(row):
    return jnp.transpose(jnp.broadcast_to(row, (LANES, row.shape[1])))


def dispatch_kernel(ranks_hbm, points_hbm, out_ref, ranks_ref, points_ref, ranks_sem, points_sem):
    clouds, length, width = points_ref.shape
    devices, _, capacity, _ = out_ref.shape
    ranks_copy = pltpu.make_async_copy(ranks_hbm, ranks_ref, ranks_sem)
    ranks_copy.start()
    copies = [
        pltpu.make_async_copy(points_hbm.at[c], points_ref.at[c], points_sem.at[c])
        for c in range(clouds)
    ]
    for copy in copies:
        copy.start()
    before = (
        lax.broadcasted_iota(jnp.int32, (length, length), 0)
        < lax.broadcasted_iota(jnp.int32, (length, length), 1)
    ).astype(F32).astype(BF16)
    ranks_copy.wait()
    ranks = ranks_ref[...]
    target = ranks // length
    local = ranks - target * length
    for c in range(clouds):
        goes = lax.broadcasted_iota(jnp.int32, (devices, length), 0) == target[c : c + 1]
        ones = goes.astype(F32)
        earlier = dot(ones.astype(BF16), before)
        slot = jnp.sum(earlier * ones, axis=0, keepdims=True).astype(jnp.int32)
        where_to = target[c : c + 1] * capacity + slot
        pick = (
            lax.broadcasted_iota(jnp.int32, (devices * capacity, length), 0) == where_to
        ).astype(F32).astype(BF16)
        places = column((local[c : c + 1] + 1).astype(F32)).astype(BF16)
        marks = dot(pick, places).astype(BF16)
        out_ref[:, c, :, width:] = marks.reshape(devices, capacity, LANES)
        copies[c].wait()
        rows = dot(pick, points_ref[c]).astype(BF16)
        out_ref[:, c, :, :width] = rows.reshape(devices, capacity, width)


def place_kernel(arrived_ref, tags_ref, block_ref):
    devices, clouds, capacity, _ = arrived_ref.shape
    length, width = block_ref.shape[1] - TAG_ROWS, block_ref.shape[2]
    slots = devices * capacity
    here = lax.broadcasted_iota(jnp.int32, (slots, length), 1).astype(F32) + 1.0
    for c in range(clouds):
        rows = arrived_ref[:, c, :, :width].reshape(slots, width)
        marks = arrived_ref[:, c, :, width:].reshape(slots, LANES).astype(F32)
        wide_marks = jnp.concatenate([marks] * (length // LANES), axis=1)
        put = (wide_marks == here).astype(F32).astype(BF16)
        block_ref[c, :length] = dot(put, rows, ((0,), (0,))).astype(BF16)
        tag_row = jnp.concatenate(
            [tags_ref[c : c + 1].astype(F32) + 1.0, jnp.zeros((1, width - length), F32)], axis=1
        )
        block_ref[c, length:] = jnp.broadcast_to(tag_row, (TAG_ROWS, width)).astype(BF16)


def tags_of(block, length):
    return block[length:, :length].astype(F32)[:1]


def own_kernel(
    own_ref, w_ref, w_out_ref, cot_ref, query_ref, w_kv_ref, out_copy_ref, cot_copy_ref, mixed_ref, total_ref, peak_ref
):
    clouds, length, width = query_ref.shape
    head = width // HEADS
    first = lax.broadcasted_iota(jnp.int32, (length, LANES), 1) < head
    ones = jnp.ones((length, LANES), BF16)
    scale = head ** (-0.5) * LOG2E
    for c in range(clouds):
        projected = dot(normalize(own_ref[c, :length].astype(F32)), w_ref[...]).astype(BF16)
        query_ref[c] = projected[:, :width]
        tags = tags_of(own_ref[c], length)
        allowed = jnp.concatenate([column(tags)] * (length // LANES), axis=1) == tags
        for h in range(width // LANES):
            lanes = slice(h * LANES, (h + 1) * LANES)
            queries = projected[:, lanes]
            keys = projected[:, width:][:, lanes]
            values = jnp.concatenate([projected[:, 2 * width :][:, lanes], ones], axis=1)
            peaks, sums = [], []
            for inside in (first, ~first):
                asked = jnp.where(inside, queries, jnp.zeros_like(queries))
                scores = jnp.where(allowed, dot(asked, keys, ((1,), (1,))), -1e30)
                peak = jnp.max(scores, axis=1, keepdims=True)
                sums.append(dot(jnp.exp2((scores - peak) * scale).astype(BF16), values))
                peaks.append(peak)
            mixed_ref[c, :, lanes] = jnp.where(first, sums[0][:, :LANES], sums[1][:, :LANES])
            total_ref[c, :, lanes] = jnp.where(first, sums[0][:, LANES:], sums[1][:, LANES:])
            peak_ref[c, :, lanes] = jnp.where(first, peaks[0], peaks[1])
    w_kv_ref[...] = w_ref[:, width:]
    out_copy_ref[...] = w_out_ref[...]
    cot_copy_ref[...] = cot_ref[...]


def halo_kernel(
    own_ref, low_ref, high_ref, query_ref, w_ref, w_out_ref, mixed_ref, total_ref, peak_ref, res_ref, normed_ref
):
    clouds, length, width = query_ref.shape
    head = width // HEADS
    first = lax.broadcasted_iota(jnp.int32, (length, LANES), 1) < head
    ones = jnp.ones((length, LANES), BF16)
    scale = head ** (-0.5) * LOG2E
    for c in range(clouds):
        sides = []
        for ref in (low_ref, high_ref):
            normed = normalize(ref[c, :length].astype(F32))
            sides.append((dot(normed, w_ref[...]).astype(BF16), tags_of(ref[c], length)))
        asks = column(tags_of(own_ref[c], length))
        asks = jnp.concatenate([asks] * (length // LANES), axis=1)
        allowed = [asks == tags for _, tags in sides]
        for h in range(width // LANES):
            lanes = slice(h * LANES, (h + 1) * LANES)
            values = slice(width + h * LANES, width + (h + 1) * LANES)
            queries = query_ref[c, :, lanes]
            old_peak = peak_ref[c, :, lanes]
            peaks, sums = [], []
            for k, inside in enumerate((first, ~first)):
                asked = jnp.where(inside, queries, jnp.zeros_like(queries))
                scores = [
                    jnp.where(ok, dot(asked, kv[:, lanes], ((1,), (1,))), -1e30)
                    for (kv, _), ok in zip(sides, allowed)
                ]
                best = jnp.max(jnp.maximum(scores[0], scores[1]), axis=1, keepdims=True)
                best = jnp.maximum(best, old_peak[:, k * head : k * head + 1])
                part = None
                for (kv, _), s in zip(sides, scores):
                    weights = jnp.exp2((s - best) * scale).astype(BF16)
                    add = dot(weights, jnp.concatenate([kv[:, values], ones], axis=1))
                    part = add if part is None else part + add
                sums.append(part)
                peaks.append(best)
            fade = jnp.exp2((old_peak - jnp.where(first, peaks[0], peaks[1])) * scale)
            above = jnp.where(first, sums[0][:, :LANES], sums[1][:, :LANES])
            under = jnp.where(first, sums[0][:, LANES:], sums[1][:, LANES:])
            above += mixed_ref[c, :, lanes] * fade
            under += total_ref[c, :, lanes] * fade
            part = dot((above / under).astype(BF16), w_out_ref[lanes, :])
            attended = part if h == 0 else attended + part
        residual = (own_ref[c, :length].astype(F32) + attended).astype(BF16)
        rows = slice(c * length, (c + 1) * length)
        res_ref[rows] = residual
        normed_ref[rows] = normalize(residual.astype(F32))


def up_kernel(parity_ref, normed_ref, w_up_ref, cot_ref, hidden_ref, grad_ref):
    blocks, _, units, _ = w_up_ref.shape
    parity = parity_ref[0]
    half = units // 2
    for j in range(0, blocks, 2):
        weights = w_up_ref[j : j + 2, parity].reshape(2 * units, -1)
        product = dot(weights, normed_ref[...], ((1,), (1,)))
        hidden = jax.nn.gelu(product).astype(BF16)
        hidden_ref[j * units : (j + 2) * units] = hidden
        grad = dot(hidden, cot_ref[...]).astype(BF16)
        for k in range(2):
            grad_ref[0, j + k] = grad[k * units : k * units + half]
            grad_ref[1, j + k] = grad[k * units + half : (k + 1) * units]


def down_kernel(parity_ref, res_ref, one_ref, two_ref, w_ref, out_ref):
    blocks, _, units, width = w_ref.shape
    parity = parity_ref[0]
    total = dot(one_ref[...], w_ref[:, parity].reshape(blocks * units, width), ((0,), (0,)))
    total += dot(two_ref[...], w_ref[:, 1 - parity].reshape(blocks * units, width), ((0,), (0,)))
    out_ref[...] = (res_ref[...].astype(F32) + total).astype(BF16)


VMEM = pl.BlockSpec(memory_space=pltpu.VMEM)
SMEM = pl.BlockSpec(memory_space=pltpu.SMEM)
ANY = pl.BlockSpec(memory_space=pl.ANY)


def call(kernel, outs, specs, args, scratch=(), flops=0, out_spec=VMEM, limit=SMALL):
    return pl.pallas_call(
        kernel,
        out_shape=[jax.ShapeDtypeStruct(shape, kind) for shape, kind in outs],
        in_specs=specs,
        out_specs=[out_spec] * len(outs),
        scratch_shapes=list(scratch),
        compiler_params=pltpu.CompilerParams(vmem_limit_bytes=limit),
        cost_estimate=pl.CostEstimate(
            flops=flops, bytes_accessed=sum(4 * math.prod(s) for s, _ in outs), transcendentals=0
        ),
    )(*args)


def on_device(points, hilbert_rank, patch_id, w_qkv, w_out, w_up, w_down, cotangent):
    clouds, length, width = points.shape[1:]
    rows_all = clouds * length
    devices = lax.axis_size("point")
    groups = lax.axis_size("dp")
    units = w_up.shape[0]
    capacity = 2 * length // devices
    me = lax.axis_index("point")
    parity = (me & 1).reshape(1).astype(jnp.int32)
    up_all = lax.all_gather(w_up, "point", axis=0, tiled=True)
    down_all = lax.all_gather(w_down, "point", axis=0, tiled=True)

    forward = [(i, i + 1) for i in range(devices - 1)]
    backward = [(i + 1, i) for i in range(devices - 1)]
    dma = pltpu.SemaphoreType.DMA
    (outgoing,) = call(
        dispatch_kernel,
        [((devices, clouds, capacity, width + LANES), BF16)],
        [ANY, ANY],
        (hilbert_rank[0], points[0]),
        (
            pltpu.VMEM((clouds, length), jnp.int32),
            pltpu.VMEM((clouds, length, width), BF16),
            dma,
            dma((clouds,)),
        ),
        flops=2 * rows_all * devices * capacity * width,
        limit=LARGE,
    )
    arrived = lax.all_to_all(outgoing, "point", 0, 0, tiled=True)
    block = (clouds, length + TAG_ROWS, width)
    (own,) = call(
        place_kernel,
        [(block, BF16)],
        [VMEM, VMEM],
        (arrived, patch_id[0]),
        flops=2 * rows_all * width * devices * capacity,
    )
    low = lax.ppermute(own, "point", forward)
    high = lax.ppermute(own, "point", backward)
    each = (clouds, length, width)
    flat = (rows_all, width)
    query, w_kv, w_out, cot_rows, *sums = call(
        own_kernel,
        [(each, BF16), ((width, 2 * width), BF16), ((width, width), BF16), (flat, BF16)] + [(each, F32)] * 3,
        [VMEM] * 4,
        (own, w_qkv, w_out, cotangent[0].reshape(flat)),
        flops=2 * rows_all * width * (3 * width + 4 * length),
    )

    blocks = devices // 2
    up_blocks = up_all.reshape(blocks, 2, units, width)
    halves = [(blocks * units, rows_all), (2, blocks, units // 2, width)]
    residual, normed_two = call(
        halo_kernel,
        [(flat, BF16), (flat, BF16)],
        [VMEM] * 9,
        (own, low, high, query, w_kv, w_out, *sums),
        flops=2 * rows_all * width * (5 * width + 8 * length),
    )
    up = partial(
        call,
        up_kernel,
        [(shape, BF16) for shape in halves],
        [SMEM] + [VMEM] * 3,
        flops=4 * rows_all * width * units * blocks,
    )
    hidden_two, grad_two = up((1 - parity, normed_two, up_blocks, cot_rows))
    grad_got = lax.ppermute(grad_two, "point", [(i, i ^ 1) for i in range(devices)])
    hidden_one, grad_one = up((parity, normed_two, up_blocks, cot_rows))
    grad = (grad_one.astype(F32) + grad_got.astype(F32)).astype(BF16)
    grad = grad.reshape(2 * blocks, units // 2, width)

    stages = groups // 2
    planes = [
        [(z * 2 + h) * devices + j * 2 + core for h in range(2) for j in range(blocks)]
        for z in range(stages)
        for core in range(2)
    ]
    grad = lax.all_to_all(
        grad, ("dp", "point"), 0, 0, axis_index_groups=planes, tiled=True
    )
    grad = jnp.sum(grad.astype(F32), axis=0).astype(BF16)
    piece = units // groups
    grad = lax.all_to_all(
        grad.reshape(stages, piece, width),
        "dp",
        0,
        0,
        axis_index_groups=[[z * 2 + h for z in range(stages)] for h in range(2)],
        tiled=True,
    )
    grad = jnp.sum(grad.astype(F32), axis=0).astype(BF16)
    grad = lax.all_to_all(
        jnp.broadcast_to(grad[None], (groups, piece, width)), "dp", 0, 0, tiled=True
    )
    grad = grad.reshape(stages, 2, piece, width).transpose(1, 0, 2, 3).reshape(units, width)
    grad_down = grad.astype(F32)

    (layer_out,) = call(
        down_kernel,
        [(flat, BF16)],
        [SMEM] + [VMEM] * 4,
        (parity, residual, hidden_one, hidden_two, down_all.reshape(blocks, 2, units, width)),
        flops=2 * rows_all * width * devices * units,
    )
    return layer_out.reshape(1, clouds, length, width), grad_down


def solution(mesh):
    placed = (
        P("dp", None, "point", None),
        P("dp", None, "point"),
        P("dp", None, "point"),
        P(),
        P(),
        P("point", None),
        P("point", None),
        P("dp", None, "point", None),
    )
    return jax.shard_map(
        on_device,
        mesh=mesh,
        in_specs=placed,
        out_specs=(P("dp", None, "point", None), P("point", None)),
        check_vma=False,
    )
```

```python
import math
from functools import partial

import jax
import jax.numpy as jnp
from jax import lax
from jax.experimental import pallas as pl
from jax.experimental.pallas import tpu as pltpu
from jax.sharding import PartitionSpec as P

HEADS = 8
LANES = 128
TAG_ROWS = 16
LOG2E = math.log2(math.e)
SMALL = 16 * 1024 * 1024
LARGE = 60 * 1024 * 1024
F32 = jnp.float32
BF16 = jnp.bfloat16


def dot(a, b, dims=((1,), (0,))):
    return lax.dot_general(a, b, (dims, ((), ())), preferred_element_type=F32)


def normalize(wide):
    centre = jnp.mean(wide, axis=-1, keepdims=True)
    spread = jnp.mean(jnp.square(wide - centre), axis=-1, keepdims=True)
    return ((wide - centre) * lax.rsqrt(spread + 1e-05)).astype(BF16)


def column(row):
    return jnp.transpose(jnp.broadcast_to(row, (LANES, row.shape[1])))


def dispatch_kernel(ranks_hbm, points_hbm, out_ref, ranks_ref, points_ref, ranks_sem, points_sem):
    clouds, length, width = points_ref.shape
    devices, _, capacity, _ = out_ref.shape
    ranks_copy = pltpu.make_async_copy(ranks_hbm, ranks_ref, ranks_sem)
    ranks_copy.start()
    copies = [
        pltpu.make_async_copy(points_hbm.at[c], points_ref.at[c], points_sem.at[c])
        for c in range(clouds)
    ]
    for copy in copies:
        copy.start()
    before = (
        lax.broadcasted_iota(jnp.int32, (length, length), 0)
        < lax.broadcasted_iota(jnp.int32, (length, length), 1)
    ).astype(F32).astype(BF16)
    ranks_copy.wait()
    ranks = ranks_ref[...]
    target = ranks // length
    local = ranks - target * length
    for c in range(clouds):
        goes = lax.broadcasted_iota(jnp.int32, (devices, length), 0) == target[c : c + 1]
        ones = goes.astype(F32)
        earlier = dot(ones.astype(BF16), before)
        slot = jnp.sum(earlier * ones, axis=0, keepdims=True).astype(jnp.int32)
        where_to = target[c : c + 1] * capacity + slot
        pick = (
            lax.broadcasted_iota(jnp.int32, (devices * capacity, length), 0) == where_to
        ).astype(F32).astype(BF16)
        places = column((local[c : c + 1] + 1).astype(F32)).astype(BF16)
        marks = dot(pick, places).astype(BF16)
        out_ref[:, c, :, width:] = marks.reshape(devices, capacity, LANES)
        copies[c].wait()
        rows = dot(pick, points_ref[c]).astype(BF16)
        out_ref[:, c, :, :width] = rows.reshape(devices, capacity, width)


def place_kernel(arrived_ref, tags_ref, block_ref):
    devices, clouds, capacity, _ = arrived_ref.shape
    length, width = block_ref.shape[1] - TAG_ROWS, block_ref.shape[2]
    slots = devices * capacity
    here = lax.broadcasted_iota(jnp.int32, (slots, length), 1).astype(F32) + 1.0
    for c in range(clouds):
        rows = arrived_ref[:, c, :, :width].reshape(slots, width)
        marks = arrived_ref[:, c, :, width:].reshape(slots, LANES).astype(F32)
        wide_marks = jnp.concatenate([marks] * (length // LANES), axis=1)
        put = (wide_marks == here).astype(F32).astype(BF16)
        block_ref[c, :length] = dot(put, rows, ((0,), (0,))).astype(BF16)
        tag_row = jnp.concatenate(
            [tags_ref[c : c + 1].astype(F32) + 1.0, jnp.zeros((1, width - length), F32)], axis=1
        )
        block_ref[c, length:] = jnp.broadcast_to(tag_row, (TAG_ROWS, width)).astype(BF16)


def tags_of(block, length):
    return block[length:, :length].astype(F32)[:1]


def own_kernel(
    own_ref, w_ref, w_out_ref, cot_ref, query_ref, w_kv_ref, out_copy_ref, cot_copy_ref, mixed_ref, total_ref, peak_ref
):
    clouds, length, width = query_ref.shape
    head = width // HEADS
    first = lax.broadcasted_iota(jnp.int32, (length, LANES), 1) < head
    ones = jnp.ones((length, LANES), BF16)
    scale = head ** (-0.5) * LOG2E
    for c in range(clouds):
        projected = dot(normalize(own_ref[c, :length].astype(F32)), w_ref[...]).astype(BF16)
        query_ref[c] = projected[:, :width]
        tags = tags_of(own_ref[c], length)
        allowed = jnp.concatenate([column(tags)] * (length // LANES), axis=1) == tags
        for h in range(width // LANES):
            lanes = slice(h * LANES, (h + 1) * LANES)
            queries = projected[:, lanes]
            keys = projected[:, width:][:, lanes]
            values = jnp.concatenate([projected[:, 2 * width :][:, lanes], ones], axis=1)
            peaks, sums = [], []
            for inside in (first, ~first):
                asked = jnp.where(inside, queries, jnp.zeros_like(queries))
                scores = jnp.where(allowed, dot(asked, keys, ((1,), (1,))), -1e30)
                peak = jnp.max(scores, axis=1, keepdims=True)
                sums.append(dot(jnp.exp2((scores - peak) * scale).astype(BF16), values))
                peaks.append(peak)
            mixed_ref[c, :, lanes] = jnp.where(first, sums[0][:, :LANES], sums[1][:, :LANES])
            total_ref[c, :, lanes] = jnp.where(first, sums[0][:, LANES:], sums[1][:, LANES:])
            peak_ref[c, :, lanes] = jnp.where(first, peaks[0], peaks[1])
    w_kv_ref[...] = w_ref[:, width:]
    out_copy_ref[...] = w_out_ref[...]
    cot_copy_ref[...] = cot_ref[...]


def halo_kernel(
    own_ref, low_ref, high_ref, query_ref, w_ref, w_out_ref, mixed_ref, total_ref, peak_ref, res_ref
):
    clouds, length, width = query_ref.shape
    head = width // HEADS
    first = lax.broadcasted_iota(jnp.int32, (length, LANES), 1) < head
    ones = jnp.ones((length, LANES), BF16)
    scale = head ** (-0.5) * LOG2E
    for c in range(clouds):
        sides = []
        for ref in (low_ref, high_ref):
            normed = normalize(ref[c, :length].astype(F32))
            sides.append((dot(normed, w_ref[...]).astype(BF16), tags_of(ref[c], length)))
        asks = column(tags_of(own_ref[c], length))
        asks = jnp.concatenate([asks] * (length // LANES), axis=1)
        allowed = [asks == tags for _, tags in sides]
        for h in range(width // LANES):
            lanes = slice(h * LANES, (h + 1) * LANES)
            values = slice(width + h * LANES, width + (h + 1) * LANES)
            queries = query_ref[c, :, lanes]
            old_peak = peak_ref[c, :, lanes]
            peaks, sums = [], []
            for k, inside in enumerate((first, ~first)):
                asked = jnp.where(inside, queries, jnp.zeros_like(queries))
                scores = [
                    jnp.where(ok, dot(asked, kv[:, lanes], ((1,), (1,))), -1e30)
                    for (kv, _), ok in zip(sides, allowed)
                ]
                best = jnp.max(jnp.maximum(scores[0], scores[1]), axis=1, keepdims=True)
                best = jnp.maximum(best, old_peak[:, k * head : k * head + 1])
                part = None
                for (kv, _), s in zip(sides, scores):
                    weights = jnp.exp2((s - best) * scale).astype(BF16)
                    add = dot(weights, jnp.concatenate([kv[:, values], ones], axis=1))
                    part = add if part is None else part + add
                sums.append(part)
                peaks.append(best)
            fade = jnp.exp2((old_peak - jnp.where(first, peaks[0], peaks[1])) * scale)
            above = jnp.where(first, sums[0][:, :LANES], sums[1][:, :LANES])
            under = jnp.where(first, sums[0][:, LANES:], sums[1][:, LANES:])
            above += mixed_ref[c, :, lanes] * fade
            under += total_ref[c, :, lanes] * fade
            part = dot((above / under).astype(BF16), w_out_ref[lanes, :])
            attended = part if h == 0 else attended + part
        residual = (own_ref[c, :length].astype(F32) + attended).astype(BF16)
        res_ref[c * length : (c + 1) * length] = residual


def up_kernel(parity_ref, res_ref, w_up_ref, cot_ref, hidden_ref, grad_ref):
    blocks, _, units, _ = w_up_ref.shape
    parity = parity_ref[0]
    half = units // 2
    normed = normalize(res_ref[...].astype(F32))
    for j in range(0, blocks, 2):
        weights = w_up_ref[j : j + 2, parity].reshape(2 * units, -1)
        product = dot(weights, normed, ((1,), (1,)))
        hidden = jax.nn.gelu(product).astype(BF16)
        hidden_ref[j * units : (j + 2) * units] = hidden
        grad = dot(hidden, cot_ref[...]).astype(BF16)
        for k in range(2):
            grad_ref[0, j + k] = grad[k * units : k * units + half]
            grad_ref[1, j + k] = grad[k * units + half : (k + 1) * units]


def down_kernel(parity_ref, res_ref, one_ref, two_ref, w_ref, out_ref):
    blocks, _, units, width = w_ref.shape
    parity = parity_ref[0]
    total = dot(one_ref[...], w_ref[:, parity].reshape(blocks * units, width), ((0,), (0,)))
    total += dot(two_ref[...], w_ref[:, 1 - parity].reshape(blocks * units, width), ((0,), (0,)))
    out_ref[...] = (res_ref[...].astype(F32) + total).astype(BF16)


VMEM = pl.BlockSpec(memory_space=pltpu.VMEM)
SMEM = pl.BlockSpec(memory_space=pltpu.SMEM)
ANY = pl.BlockSpec(memory_space=pl.ANY)


def call(kernel, outs, specs, args, scratch=(), flops=0, out_spec=VMEM, limit=SMALL):
    return pl.pallas_call(
        kernel,
        out_shape=[jax.ShapeDtypeStruct(shape, kind) for shape, kind in outs],
        in_specs=specs,
        out_specs=[out_spec] * len(outs),
        scratch_shapes=list(scratch),
        compiler_params=pltpu.CompilerParams(vmem_limit_bytes=limit),
        cost_estimate=pl.CostEstimate(
            flops=flops, bytes_accessed=sum(4 * math.prod(s) for s, _ in outs), transcendentals=0
        ),
    )(*args)


def on_device(points, hilbert_rank, patch_id, w_qkv, w_out, w_up, w_down, cotangent):
    clouds, length, width = points.shape[1:]
    rows_all = clouds * length
    devices = lax.axis_size("point")
    groups = lax.axis_size("dp")
    units = w_up.shape[0]
    capacity = 2 * length // devices
    me = lax.axis_index("point")
    parity = (me & 1).reshape(1).astype(jnp.int32)
    up_all = lax.all_gather(w_up, "point", axis=0, tiled=True)
    down_all = lax.all_gather(w_down, "point", axis=0, tiled=True)

    forward = [(i, i + 1) for i in range(devices - 1)]
    backward = [(i + 1, i) for i in range(devices - 1)]
    dma = pltpu.SemaphoreType.DMA
    (outgoing,) = call(
        dispatch_kernel,
        [((devices, clouds, capacity, width + LANES), BF16)],
        [ANY, ANY],
        (hilbert_rank[0], points[0]),
        (
            pltpu.VMEM((clouds, length), jnp.int32),
            pltpu.VMEM((clouds, length, width), BF16),
            dma,
            dma((clouds,)),
        ),
        flops=2 * rows_all * devices * capacity * width,
        limit=LARGE,
    )
    arrived = lax.all_to_all(outgoing, "point", 0, 0, tiled=True)
    block = (clouds, length + TAG_ROWS, width)
    (own,) = call(
        place_kernel,
        [(block, BF16)],
        [VMEM, VMEM],
        (arrived, patch_id[0]),
        flops=2 * rows_all * width * devices * capacity,
    )
    low = lax.ppermute(own, "point", forward)
    high = lax.ppermute(own, "point", backward)
    each = (clouds, length, width)
    flat = (rows_all, width)
    query, w_kv, w_out, cot_rows, *sums = call(
        own_kernel,
        [(each, BF16), ((width, 2 * width), BF16), ((width, width), BF16), (flat, BF16)] + [(each, F32)] * 3,
        [VMEM] * 4,
        (own, w_qkv, w_out, cotangent[0].reshape(flat)),
        flops=2 * rows_all * width * (3 * width + 4 * length),
    )

    blocks = devices // 2
    up_blocks = up_all.reshape(blocks, 2, units, width)
    halves = [(blocks * units, rows_all), (2, blocks, units // 2, width)]
    (residual,) = call(
        halo_kernel,
        [(flat, BF16)],
        [VMEM] * 9,
        (own, low, high, query, w_kv, w_out, *sums),
        flops=2 * rows_all * width * (5 * width + 8 * length),
    )
    up = partial(
        call,
        up_kernel,
        [(shape, BF16) for shape in halves],
        [SMEM] + [VMEM] * 3,
        flops=4 * rows_all * width * units * blocks,
    )
    hidden_two, grad_two = up((1 - parity, residual, up_blocks, cot_rows))
    grad_got = lax.ppermute(grad_two, "point", [(i, i ^ 1) for i in range(devices)])
    hidden_one, grad_one = up((parity, residual, up_blocks, cot_rows))
    grad = (grad_one.astype(F32) + grad_got.astype(F32)).astype(BF16)
    grad = grad.reshape(2 * blocks, units // 2, width)

    stages = groups // 2
    planes = [
        [(z * 2 + h) * devices + j * 2 + core for h in range(2) for j in range(blocks)]
        for z in range(stages)
        for core in range(2)
    ]
    grad = lax.all_to_all(
        grad, ("dp", "point"), 0, 0, axis_index_groups=planes, tiled=True
    )
    grad = jnp.sum(grad.astype(F32), axis=0).astype(BF16)
    piece = units // groups
    grad = lax.all_to_all(
        grad.reshape(stages, piece, width),
        "dp",
        0,
        0,
        axis_index_groups=[[z * 2 + h for z in range(stages)] for h in range(2)],
        tiled=True,
    )
    grad = jnp.sum(grad.astype(F32), axis=0).astype(BF16)
    grad = lax.all_to_all(
        jnp.broadcast_to(grad[None], (groups, piece, width)), "dp", 0, 0, tiled=True
    )
    grad = grad.reshape(stages, 2, piece, width).transpose(1, 0, 2, 3).reshape(units, width)
    grad_down = grad.astype(F32)

    (layer_out,) = call(
        down_kernel,
        [(flat, BF16)],
        [SMEM] + [VMEM] * 4,
        (parity, residual, hidden_one, hidden_two, down_all.reshape(blocks, 2, units, width)),
        flops=2 * rows_all * width * devices * units,
    )
    return layer_out.reshape(1, clouds, length, width), grad_down


def solution(mesh):
    placed = (
        P("dp", None, "point", None),
        P("dp", None, "point"),
        P("dp", None, "point"),
        P(),
        P(),
        P("point", None),
        P("point", None),
        P("dp", None, "point", None),
    )
    return jax.shard_map(
        on_device,
        mesh=mesh,
        in_specs=placed,
        out_specs=(P("dp", None, "point", None), P("point", None)),
        check_vma=False,
    )
```

```python
import math
from functools import partial

import jax
import jax.numpy as jnp
from jax import lax
from jax.experimental import pallas as pl
from jax.experimental.pallas import tpu as pltpu
from jax.sharding import PartitionSpec as P

HEADS = 8
LANES = 128
TAG_ROWS = 16
LOG2E = math.log2(math.e)
SMALL = 16 * 1024 * 1024
LARGE = 60 * 1024 * 1024
F32 = jnp.float32
BF16 = jnp.bfloat16


def dot(a, b, dims=((1,), (0,))):
    return lax.dot_general(a, b, (dims, ((), ())), preferred_element_type=F32)


def normalize(wide):
    centre = jnp.mean(wide, axis=-1, keepdims=True)
    spread = jnp.mean(jnp.square(wide - centre), axis=-1, keepdims=True)
    return ((wide - centre) * lax.rsqrt(spread + 1e-05)).astype(BF16)


def column(row):
    return jnp.transpose(jnp.broadcast_to(row, (LANES, row.shape[1])))


def dispatch_kernel(ranks_hbm, points_hbm, out_ref, ranks_ref, points_ref, ranks_sem, points_sem):
    clouds, length, width = points_ref.shape
    devices, _, capacity, _ = out_ref.shape
    ranks_copy = pltpu.make_async_copy(ranks_hbm, ranks_ref, ranks_sem)
    ranks_copy.start()
    copies = [
        pltpu.make_async_copy(points_hbm.at[c], points_ref.at[c], points_sem.at[c])
        for c in range(clouds)
    ]
    for copy in copies:
        copy.start()
    before = (
        lax.broadcasted_iota(jnp.int32, (length, length), 0)
        < lax.broadcasted_iota(jnp.int32, (length, length), 1)
    ).astype(F32).astype(BF16)
    ranks_copy.wait()
    ranks = ranks_ref[...]
    target = ranks // length
    local = ranks - target * length
    for c in range(clouds):
        goes = lax.broadcasted_iota(jnp.int32, (devices, length), 0) == target[c : c + 1]
        ones = goes.astype(F32)
        earlier = dot(ones.astype(BF16), before)
        slot = jnp.sum(earlier * ones, axis=0, keepdims=True).astype(jnp.int32)
        where_to = target[c : c + 1] * capacity + slot
        pick = (
            lax.broadcasted_iota(jnp.int32, (devices * capacity, length), 0) == where_to
        ).astype(F32).astype(BF16)
        places = column((local[c : c + 1] + 1).astype(F32)).astype(BF16)
        marks = dot(pick, places).astype(BF16)
        out_ref[:, c, :, width:] = marks.reshape(devices, capacity, LANES)
        copies[c].wait()
        rows = dot(pick, points_ref[c]).astype(BF16)
        out_ref[:, c, :, :width] = rows.reshape(devices, capacity, width)


def place_kernel(arrived_ref, tags_ref, block_ref):
    devices, clouds, capacity, _ = arrived_ref.shape
    length, width = block_ref.shape[1] - TAG_ROWS, block_ref.shape[2]
    slots = devices * capacity
    here = lax.broadcasted_iota(jnp.int32, (slots, length), 1).astype(F32) + 1.0
    for c in range(clouds):
        rows = arrived_ref[:, c, :, :width].reshape(slots, width)
        marks = arrived_ref[:, c, :, width:].reshape(slots, LANES).astype(F32)
        wide_marks = jnp.concatenate([marks] * (length // LANES), axis=1)
        put = (wide_marks == here).astype(F32).astype(BF16)
        block_ref[c, :length] = dot(put, rows, ((0,), (0,))).astype(BF16)
        tag_row = jnp.concatenate(
            [tags_ref[c : c + 1].astype(F32) + 1.0, jnp.zeros((1, width - length), F32)], axis=1
        )
        block_ref[c, length:] = jnp.broadcast_to(tag_row, (TAG_ROWS, width)).astype(BF16)


def tags_of(block, length):
    return block[length:, :length].astype(F32)[:1]


def own_kernel(
    own_ref, w_ref, w_out_ref, cot_ref, query_ref, w_kv_ref, out_copy_ref, cot_copy_ref, mixed_ref, total_ref, peak_ref
):
    clouds, length, width = query_ref.shape
    head = width // HEADS
    first = lax.broadcasted_iota(jnp.int32, (length, LANES), 1) < head
    ones = jnp.ones((length, LANES), BF16)
    scale = head ** (-0.5) * LOG2E
    for c in range(clouds):
        projected = dot(normalize(own_ref[c, :length].astype(F32)), w_ref[...]).astype(BF16)
        query_ref[c] = projected[:, :width]
        tags = tags_of(own_ref[c], length)
        allowed = jnp.concatenate([column(tags)] * (length // LANES), axis=1) == tags
        for h in range(width // LANES):
            lanes = slice(h * LANES, (h + 1) * LANES)
            queries = projected[:, lanes]
            keys = projected[:, width:][:, lanes]
            values = jnp.concatenate([projected[:, 2 * width :][:, lanes], ones], axis=1)
            peaks, sums = [], []
            for inside in (first, ~first):
                asked = jnp.where(inside, queries, jnp.zeros_like(queries))
                scores = jnp.where(allowed, dot(asked, keys, ((1,), (1,))), -1e30)
                peak = jnp.max(scores, axis=1, keepdims=True)
                sums.append(dot(jnp.exp2((scores - peak) * scale).astype(BF16), values))
                peaks.append(peak)
            mixed_ref[c, :, lanes] = jnp.where(first, sums[0][:, :LANES], sums[1][:, :LANES])
            total_ref[c, :, lanes] = jnp.where(first, sums[0][:, LANES:], sums[1][:, LANES:])
            peak_ref[c, :, lanes] = jnp.where(first, peaks[0], peaks[1])
    w_kv_ref[...] = w_ref[:, width:]
    out_copy_ref[...] = w_out_ref[...]
    cot_copy_ref[...] = cot_ref[...]


def low_kernel(
    own_ref, low_ref, query_ref, w_ref, mixed_ref, total_ref, peak_ref, mixed_out, total_out, peak_out
):
    clouds, length, width = query_ref.shape
    head = width // HEADS
    first = lax.broadcasted_iota(jnp.int32, (length, LANES), 1) < head
    ones = jnp.ones((length, LANES), BF16)
    scale = head ** (-0.5) * LOG2E
    for c in range(clouds):
        sides = []
        for ref in (low_ref,):
            normed = normalize(ref[c, :length].astype(F32))
            sides.append((dot(normed, w_ref[...]).astype(BF16), tags_of(ref[c], length)))
        asks = column(tags_of(own_ref[c], length))
        asks = jnp.concatenate([asks] * (length // LANES), axis=1)
        allowed = [asks == tags for _, tags in sides]
        for h in range(width // LANES):
            lanes = slice(h * LANES, (h + 1) * LANES)
            values = slice(width + h * LANES, width + (h + 1) * LANES)
            queries = query_ref[c, :, lanes]
            old_peak = peak_ref[c, :, lanes]
            peaks, sums = [], []
            for k, inside in enumerate((first, ~first)):
                asked = jnp.where(inside, queries, jnp.zeros_like(queries))
                scores = [
                    jnp.where(ok, dot(asked, kv[:, lanes], ((1,), (1,))), -1e30)
                    for (kv, _), ok in zip(sides, allowed)
                ]
                best = jnp.max(scores[0], axis=1, keepdims=True)
                best = jnp.maximum(best, old_peak[:, k * head : k * head + 1])
                part = None
                for (kv, _), s in zip(sides, scores):
                    weights = jnp.exp2((s - best) * scale).astype(BF16)
                    add = dot(weights, jnp.concatenate([kv[:, values], ones], axis=1))
                    part = add if part is None else part + add
                sums.append(part)
                peaks.append(best)
            fade = jnp.exp2((old_peak - jnp.where(first, peaks[0], peaks[1])) * scale)
            above = jnp.where(first, sums[0][:, :LANES], sums[1][:, :LANES])
            under = jnp.where(first, sums[0][:, LANES:], sums[1][:, LANES:])
            above += mixed_ref[c, :, lanes] * fade
            under += total_ref[c, :, lanes] * fade
            mixed_out[c, :, lanes] = above
            total_out[c, :, lanes] = under
            peak_out[c, :, lanes] = jnp.where(first, peaks[0], peaks[1])


def halo_kernel(
    own_ref, high_ref, query_ref, w_ref, w_out_ref, mixed_ref, total_ref, peak_ref, res_ref
):
    clouds, length, width = query_ref.shape
    head = width // HEADS
    first = lax.broadcasted_iota(jnp.int32, (length, LANES), 1) < head
    ones = jnp.ones((length, LANES), BF16)
    scale = head ** (-0.5) * LOG2E
    for c in range(clouds):
        sides = []
        for ref in (high_ref,):
            normed = normalize(ref[c, :length].astype(F32))
            sides.append((dot(normed, w_ref[...]).astype(BF16), tags_of(ref[c], length)))
        asks = column(tags_of(own_ref[c], length))
        asks = jnp.concatenate([asks] * (length // LANES), axis=1)
        allowed = [asks == tags for _, tags in sides]
        for h in range(width // LANES):
            lanes = slice(h * LANES, (h + 1) * LANES)
            values = slice(width + h * LANES, width + (h + 1) * LANES)
            queries = query_ref[c, :, lanes]
            old_peak = peak_ref[c, :, lanes]
            peaks, sums = [], []
            for k, inside in enumerate((first, ~first)):
                asked = jnp.where(inside, queries, jnp.zeros_like(queries))
                scores = [
                    jnp.where(ok, dot(asked, kv[:, lanes], ((1,), (1,))), -1e30)
                    for (kv, _), ok in zip(sides, allowed)
                ]
                best = jnp.max(scores[0], axis=1, keepdims=True)
                best = jnp.maximum(best, old_peak[:, k * head : k * head + 1])
                part = None
                for (kv, _), s in zip(sides, scores):
                    weights = jnp.exp2((s - best) * scale).astype(BF16)
                    add = dot(weights, jnp.concatenate([kv[:, values], ones], axis=1))
                    part = add if part is None else part + add
                sums.append(part)
                peaks.append(best)
            fade = jnp.exp2((old_peak - jnp.where(first, peaks[0], peaks[1])) * scale)
            above = jnp.where(first, sums[0][:, :LANES], sums[1][:, :LANES])
            under = jnp.where(first, sums[0][:, LANES:], sums[1][:, LANES:])
            above += mixed_ref[c, :, lanes] * fade
            under += total_ref[c, :, lanes] * fade
            part = dot((above / under).astype(BF16), w_out_ref[lanes, :])
            attended = part if h == 0 else attended + part
        residual = (own_ref[c, :length].astype(F32) + attended).astype(BF16)
        res_ref[c * length : (c + 1) * length] = residual


def up_kernel(parity_ref, res_ref, w_up_ref, cot_ref, hidden_ref, grad_ref):
    blocks, _, units, _ = w_up_ref.shape
    parity = parity_ref[0]
    half = units // 2
    normed = normalize(res_ref[...].astype(F32))
    for j in range(0, blocks, 2):
        weights = w_up_ref[j : j + 2, parity].reshape(2 * units, -1)
        product = dot(weights, normed, ((1,), (1,)))
        hidden = jax.nn.gelu(product).astype(BF16)
        hidden_ref[j * units : (j + 2) * units] = hidden
        grad = dot(hidden, cot_ref[...]).astype(BF16)
        for k in range(2):
            grad_ref[0, j + k] = grad[k * units : k * units + half]
            grad_ref[1, j + k] = grad[k * units + half : (k + 1) * units]


def down_kernel(parity_ref, res_ref, one_ref, two_ref, w_ref, out_ref):
    blocks, _, units, width = w_ref.shape
    parity = parity_ref[0]
    total = dot(one_ref[...], w_ref[:, parity].reshape(blocks * units, width), ((0,), (0,)))
    total += dot(two_ref[...], w_ref[:, 1 - parity].reshape(blocks * units, width), ((0,), (0,)))
    out_ref[...] = (res_ref[...].astype(F32) + total).astype(BF16)


VMEM = pl.BlockSpec(memory_space=pltpu.VMEM)
SMEM = pl.BlockSpec(memory_space=pltpu.SMEM)
ANY = pl.BlockSpec(memory_space=pl.ANY)


def call(kernel, outs, specs, args, scratch=(), flops=0, out_spec=VMEM, limit=SMALL):
    return pl.pallas_call(
        kernel,
        out_shape=[jax.ShapeDtypeStruct(shape, kind) for shape, kind in outs],
        in_specs=specs,
        out_specs=[out_spec] * len(outs),
        scratch_shapes=list(scratch),
        compiler_params=pltpu.CompilerParams(vmem_limit_bytes=limit),
        cost_estimate=pl.CostEstimate(
            flops=flops, bytes_accessed=sum(4 * math.prod(s) for s, _ in outs), transcendentals=0
        ),
    )(*args)


def on_device(points, hilbert_rank, patch_id, w_qkv, w_out, w_up, w_down, cotangent):
    clouds, length, width = points.shape[1:]
    rows_all = clouds * length
    devices = lax.axis_size("point")
    groups = lax.axis_size("dp")
    units = w_up.shape[0]
    capacity = 2 * length // devices
    me = lax.axis_index("point")
    parity = (me & 1).reshape(1).astype(jnp.int32)
    up_all = lax.all_gather(w_up, "point", axis=0, tiled=True)
    down_all = lax.all_gather(w_down, "point", axis=0, tiled=True)

    forward = [(i, i + 1) for i in range(devices - 1)]
    backward = [(i + 1, i) for i in range(devices - 1)]
    dma = pltpu.SemaphoreType.DMA
    (outgoing,) = call(
        dispatch_kernel,
        [((devices, clouds, capacity, width + LANES), BF16)],
        [ANY, ANY],
        (hilbert_rank[0], points[0]),
        (
            pltpu.VMEM((clouds, length), jnp.int32),
            pltpu.VMEM((clouds, length, width), BF16),
            dma,
            dma((clouds,)),
        ),
        flops=2 * rows_all * devices * capacity * width,
        limit=LARGE,
    )
    arrived = lax.all_to_all(outgoing, "point", 0, 0, tiled=True)
    block = (clouds, length + TAG_ROWS, width)
    (own,) = call(
        place_kernel,
        [(block, BF16)],
        [VMEM, VMEM],
        (arrived, patch_id[0]),
        flops=2 * rows_all * width * devices * capacity,
    )
    low = lax.ppermute(own, "point", forward)
    high = lax.ppermute(own, "point", backward)
    each = (clouds, length, width)
    flat = (rows_all, width)
    query, w_kv, w_out, cot_rows, *sums = call(
        own_kernel,
        [(each, BF16), ((width, 2 * width), BF16), ((width, width), BF16), (flat, BF16)] + [(each, F32)] * 3,
        [VMEM] * 4,
        (own, w_qkv, w_out, cotangent[0].reshape(flat)),
        flops=2 * rows_all * width * (3 * width + 4 * length),
    )

    blocks = devices // 2
    up_blocks = up_all.reshape(blocks, 2, units, width)
    halves = [(blocks * units, rows_all), (2, blocks, units // 2, width)]
    sums = call(
        low_kernel,
        [(each, F32)] * 3,
        [VMEM] * 7,
        (own, low, query, w_kv, *sums),
        flops=2 * rows_all * width * (2 * width + 4 * length),
    )
    (residual,) = call(
        halo_kernel,
        [(flat, BF16)],
        [VMEM] * 8,
        (own, high, query, w_kv, w_out, *sums),
        flops=2 * rows_all * width * (5 * width + 8 * length),
    )
    up = partial(
        call,
        up_kernel,
        [(shape, BF16) for shape in halves],
        [SMEM] + [VMEM] * 3,
        flops=4 * rows_all * width * units * blocks,
    )
    hidden_two, grad_two = up((1 - parity, residual, up_blocks, cot_rows))
    grad_got = lax.ppermute(grad_two, "point", [(i, i ^ 1) for i in range(devices)])
    hidden_one, grad_one = up((parity, residual, up_blocks, cot_rows))
    grad = (grad_one.astype(F32) + grad_got.astype(F32)).astype(BF16)
    grad = grad.reshape(2 * blocks, units // 2, width)

    stages = groups // 2
    planes = [
        [(z * 2 + h) * devices + j * 2 + core for h in range(2) for j in range(blocks)]
        for z in range(stages)
        for core in range(2)
    ]
    grad = lax.all_to_all(
        grad, ("dp", "point"), 0, 0, axis_index_groups=planes, tiled=True
    )
    grad = jnp.sum(grad.astype(F32), axis=0).astype(BF16)
    piece = units // groups
    grad = lax.all_to_all(
        grad.reshape(stages, piece, width),
        "dp",
        0,
        0,
        axis_index_groups=[[z * 2 + h for z in range(stages)] for h in range(2)],
        tiled=True,
    )
    grad = jnp.sum(grad.astype(F32), axis=0).astype(BF16)
    grad = lax.all_to_all(
        jnp.broadcast_to(grad[None], (groups, piece, width)), "dp", 0, 0, tiled=True
    )
    grad = grad.reshape(stages, 2, piece, width).transpose(1, 0, 2, 3).reshape(units, width)
    grad_down = grad.astype(F32)

    (layer_out,) = call(
        down_kernel,
        [(flat, BF16)],
        [SMEM] + [VMEM] * 4,
        (parity, residual, hidden_one, hidden_two, down_all.reshape(blocks, 2, units, width)),
        flops=2 * rows_all * width * devices * units,
    )
    return layer_out.reshape(1, clouds, length, width), grad_down


def solution(mesh):
    placed = (
        P("dp", None, "point", None),
        P("dp", None, "point"),
        P("dp", None, "point"),
        P(),
        P(),
        P("point", None),
        P("point", None),
        P("dp", None, "point", None),
    )
    return jax.shard_map(
        on_device,
        mesh=mesh,
        in_specs=placed,
        out_specs=(P("dp", None, "point", None), P("point", None)),
        check_vma=False,
    )
```
